256 devices in a mesh: ax: 32 (over y, z_lo, core), ay: 4 (over x), fr: 2 (over z_hi).
Axes of the slice: x: 4, y: 4, z: 8 (z_hi: 2, z_lo: 4; z = z_hi * 4 + z_lo), core: 2. Of those that a mesh axis runs over, the one named last changes fastest.
Arguments:
- echoes: float32 [128, 2, 1024, 512], P('fr', None, 'ax', 'ay'), may hold values from -6 to 6
- stolt_table: float32 [8, 128, 128], replicated, may hold values from -0.5 to 0.5
- kz_start: int32 [1024, 4], P(('ay', 'ax', 'fr')), may hold values from 0 to 1
- weight_ids: int32 [1024, 4, 2], P(('ay', 'ax', 'fr')), may hold values from 0 to 7
Outputs:
- image: float32 [2, 1024, 512, 384], P(None, ('ay', 'ax', 'fr'))
The draws below stay inside these ranges and needn't reach their ends.
All inputs are finite; a program needn't handle non-finite values.
Results may differ from the reference program's by a relative error of at most 0.0003.
Values sent between devices are 32-bit elements; how exact they have to be, the bound alone decides.
No kernel may reach another device: no remote copies, remote signals or barrier semaphores. Data moves between devices by JAX's collectives and lax.ppermute only.
A program may use at most 128 MiB of HBM per device.

```python
import jax
import jax.numpy as jnp
from jax import lax

X = 1024
Y = 512
F = 128
KB = 128
NKB = 3
BAND = 2
NW = 8
TK = 128
KZ = 384


def set_ends(drawn, key, low, largest):
    shape = drawn.shape
    place = [jax.random.randint(jax.random.fold_in(key, axis), (), 0, shape[axis]) for axis in range(len(shape))]
    drawn = drawn.at[tuple(place)].set(low)
    longest = shape.index(max(shape))
    place[longest] = (place[longest] + 1) % shape[longest]
    return drawn.at[tuple(place)].set(largest)


def level_of(key, shape, pieces, least, high):
    def one(axis_at, shards_of):
        steps = jax.random.uniform(jax.random.fold_in(jax.random.fold_in(key, 6), axis_at), (shards_of,), jnp.float32, least / len(pieces), high / len(pieces))
        return jnp.repeat(jnp.exp(steps), shape[axis_at] // shards_of).reshape((-1,) + (1,) * (len(shape) - axis_at - 1))

    level = one(*pieces[0])
    for cut in pieces[1:]:
        level = level * one(*cut)
    return level


def centred(key, dims, scale, limit, cuts=(), kind=jnp.bfloat16):
    values = jax.random.normal(key, dims, jnp.float32) * scale
    if len(cuts) > 0:
        values = level_of(key, dims, cuts, -0.22, 0.18) * values
    return jnp.clip(values, min=-limit, max=limit).astype(kind)


def setup_inputs(seed: int = 0) -> dict:
    streams_of = jax.random.split(jax.random.key(seed), 5)
    return {
        "echoes": centred(streams_of[0], (F, 2, X, Y), 1.0, 6.0, ((0, 2), (2, 32), (3, 4)), jnp.float32),
        "stolt_table": centred(streams_of[1], (NW, F, KB), F ** -0.5, 0.5, (), jnp.float32),
        "kz_start": set_ends(jax.random.randint(streams_of[2], (X, Y // TK), 0, NKB - BAND + 1), jax.random.fold_in(streams_of[2], 1), 0, NKB - BAND).astype(jnp.int32),
        "weight_ids": set_ends(jax.random.randint(streams_of[3], (X, Y // TK, BAND), 0, NW), jax.random.fold_in(streams_of[3], 1), 0, NW - 1).astype(jnp.int32),
    }


def reference(echoes, stolt_table, kz_start, weight_ids):
    complex_field = lax.complex(echoes[:, 0], echoes[:, 1])
    spectrum = jnp.fft.fft2(complex_field, axes=(1, 2), norm="ortho")
    stacked = jnp.stack([jnp.real(spectrum), jnp.imag(spectrum)], axis=1)
    row_count = min(32, X)
    block_count = X // row_count
    tile_count = Y // TK
    stacked = stacked.reshape(F, 2, block_count, row_count, tile_count, TK).transpose(2, 0, 1, 3, 4, 5)
    starts = kz_start.reshape(block_count, row_count, tile_count)
    choices_ids = weight_ids.reshape(block_count, row_count, tile_count, BAND)

    def per_block(inputs):
        spec_block, start_block, id_block = inputs
        blocks_used = stolt_table[id_block]
        banded = jnp.einsum('fcxtk,xtbfm->cxtbmk', spec_block, blocks_used, precision=lax.Precision.HIGHEST)
        offsets = jnp.arange(BAND, dtype=jnp.int32)[:, None]
        inside = jnp.arange(KB, dtype=jnp.int32)[None, :]
        positions = (start_block[:, :, None, None] + offsets) * KB + inside
        onehot = (positions[..., None] == jnp.arange(KZ, dtype=jnp.int32)).astype(jnp.float32)
        placed = jnp.einsum('cxtbmk,xtbmq->cxtkq', banded, onehot, precision=lax.Precision.HIGHEST)
        values = jnp.fft.ifft(lax.complex(placed[0], placed[1]), axis=-1, norm="ortho")
        return jnp.stack([jnp.real(values), jnp.imag(values)])

    mapped = lax.map(per_block, (stacked, starts, choices_ids))
    return mapped.transpose(1, 0, 2, 3, 4, 5).reshape(2, X, Y, KZ)
```

```python
import functools
import math

import jax
import jax.numpy as jnp
import ml_dtypes
import numpy as np
from jax import lax
from jax.experimental import pallas as pl
from jax.experimental.pallas import tpu as pltpu
from jax.sharding import PartitionSpec as P

TK = 128
KZ = 384
LANES = 128


def halves_of(table):
    high = table.astype(ml_dtypes.bfloat16)
    low = (table - high.astype(np.float64)).astype(ml_dtypes.bfloat16)
    return np.stack([high, low])


def radix4_tables(length):
    quarter = length // 4
    n = np.arange(quarter)
    tables = []
    for r in range(4):
        phase = ((4 * np.arange(quarter)[:, None] + r) * n[None, :]) % length
        angle = phase * (2.0 * math.pi / length)
        cosine, sine = np.cos(angle) / math.sqrt(length), np.sin(angle) / math.sqrt(length)
        tables.append(halves_of(np.block([[cosine, sine], [-sine, cosine]])))
    return np.stack(tables)


def inverse_table(length):
    index = np.arange(length)
    angle = (index[:, None] * index[None, :] % length) * (2.0 * math.pi / length)
    return halves_of(np.concatenate([np.cos(angle), np.sin(angle)], axis=1) / math.sqrt(length))


def split(value):
    high = value.astype(jnp.bfloat16)
    low = (value - high.astype(jnp.float32)).astype(jnp.bfloat16)
    return high, low


def dot3(left, right, contract=((1,), (0,))):
    one = functools.partial(lax.dot_general, dimension_numbers=(contract, ((), ())), preferred_element_type=jnp.float32)
    return one(left[0], right[0]) + (one(left[1], right[0]) + one(left[0], right[1]))


def radix4(pieces):
    (ar, ai), (br, bi), (cr, ci), (dr, di) = pieces
    even = (ar + cr, ai + ci)
    odd = (br + dr, bi + di)
    even_less = (ar - cr, ai - ci)
    odd_less = (br - dr, bi - di)
    return [
        (even[0] + odd[0], even[1] + odd[1]),
        (even_less[0] + odd_less[1], even_less[1] - odd_less[0]),
        (even[0] - odd[0], even[1] - odd[1]),
        (even_less[0] - odd_less[1], even_less[1] + odd_less[0]),
    ]


def weights_kernel(starts_ref, ids_ref, table_ref, inverse_ref, out_ref, high_ref, low_ref):
    step = pl.program_id(0)
    block_count, freq_count, _ = table_ref.shape
    tiles = out_ref.shape[0]

    @pl.when(step == 0)
    def _():
        for w in range(block_count):
            for f2 in range(2):
                for fr in range(2):
                    rows = table_ref[w, pl.ds(fr * (freq_count // 2) + f2, freq_count // 4, stride=2), :]
                    high, low = split(rows)
                    at = (f2 * 2 + fr) * (freq_count // 4)
                    high_ref[w, at : at + freq_count // 4, :] = high
                    low_ref[w, at : at + freq_count // 4, :] = low

    for t in range(tiles):
        tile = step * tiles + t
        first, second = ids_ref[2 * tile], ids_ref[2 * tile + 1]
        left = (
            jnp.concatenate([high_ref[first], high_ref[second]], axis=1),
            jnp.concatenate([low_ref[first], low_ref[second]], axis=1),
        )
        rows = pl.ds(pl.multiple_of(starts_ref[tile] * LANES, LANES), 2 * LANES)
        product = dot3(left, (inverse_ref[0, rows, :], inverse_ref[1, rows, :]))
        high, low = split(product)
        for c in range(2):
            at = c * freq_count
            out_ref[t, 0, at : at + freq_count, :] = high[:, c * KZ : (c + 1) * KZ]
            out_ref[t, 1, at : at + freq_count, :] = low[:, c * KZ : (c + 1) * KZ]


def tile_weights(stolt_table, kz_start, weight_ids):
    block_count, freq_count, block_width = stolt_table.shape
    kx_rows, tiles = kz_start.shape
    inverse = inverse_table(KZ)
    return pl.pallas_call(
        weights_kernel,
        grid_spec=pltpu.PrefetchScalarGridSpec(
            num_scalar_prefetch=2,
            grid=(kx_rows,),
            in_specs=[
                pl.BlockSpec(stolt_table.shape, lambda i, *_: (0, 0, 0)),
                pl.BlockSpec(inverse.shape, lambda i, *_: (0, 0, 0)),
            ],
            out_specs=pl.BlockSpec((tiles, 2, 2 * freq_count, KZ), lambda i, *_: (i, 0, 0, 0)),
            scratch_shapes=[pltpu.VMEM(stolt_table.shape, jnp.bfloat16)] * 2,
        ),
        out_shape=jax.ShapeDtypeStruct((kx_rows * tiles, 2, 2 * freq_count, KZ), jnp.bfloat16),
        compiler_params=pltpu.CompilerParams(vmem_limit_bytes=24 << 20),
        name="tile_weights",
    )(kz_start.reshape(-1), weight_ids.reshape(-1), stolt_table, jnp.asarray(inverse))


def forward_x_kernel(x_ref, table_ref, out_ref):
    sources, freqs, _, span, _ = x_ref.shape
    per = sources // 4
    quarter = per * span
    pieces = []
    for q in range(4):
        pieces.append(
            tuple(
                jnp.concatenate([x_ref[q * per : (q + 1) * per, f, c].reshape(quarter, LANES) for f in range(freqs)], axis=1)
                for c in range(2)
            )
        )
    stride = 4 * freqs * 2
    for r, (real, imag) in enumerate(radix4(pieces)):
        right = split(jnp.concatenate([real, imag], axis=0))
        product = dot3((table_ref[r, 0], table_ref[r, 1]), right)
        for c in range(2):
            for f in range(freqs):
                out_ref[pl.ds((r * freqs + f) * 2 + c, quarter, stride=stride), :] = product[
                    c * quarter : (c + 1) * quarter, f * LANES : (f + 1) * LANES
                ]


def forward_x(received):
    sources, freqs, _, span, columns = received.shape
    table = radix4_tables(sources * span)
    return pl.pallas_call(
        forward_x_kernel,
        out_shape=jax.ShapeDtypeStruct((sources * span * freqs * 2, columns), jnp.float32),
        compiler_params=pltpu.CompilerParams(vmem_limit_bytes=40 << 20),
        name="forward_x",
    )(received, jnp.asarray(table))


def image_kernel(s_ref, y_ref, w_ref, out_ref, spec_ref):
    step = pl.program_id(0)
    tiles, _, depth, _ = w_ref.shape
    freq_count = depth // 2
    ky_count = tiles * TK
    kx_rows = spec_ref.shape[1]
    rows_q = s_ref.shape[0] // 4
    message = 4 * kx_rows
    per = freq_count // 4

    @pl.when(step == 0)
    def _():
        halves = [[] for _ in range(4)]
        for r in range(kx_rows):
            pieces = []
            for q in range(4):
                parts = []
                for c in range(2):
                    loaded = [
                        s_ref[pl.ds(q * rows_q + fr * message + (r * 2 + f2) * 2 + c, per, stride=2 * message), :]
                        for f2 in range(2)
                        for fr in range(2)
                    ]
                    parts.append(jnp.concatenate(loaded, axis=0))
                pieces.append(tuple(parts))
            for residue, (real, imag) in enumerate(radix4(pieces)):
                halves[residue].append(split(jnp.concatenate([real, imag], axis=1)))
        for residue in range(4):
            right = tuple(jnp.concatenate([pair[h] for pair in halves[residue]], axis=0) for h in range(2))
            product = dot3((y_ref[residue, 0], y_ref[residue, 1]), right, ((1,), (1,)))
            for c in range(2):
                for r in range(kx_rows):
                    spec_ref[c, r, pl.ds(residue, ky_count // 4, stride=4), :] = product[
                        c * ky_count // 4 : (c + 1) * ky_count // 4, r * freq_count : (r + 1) * freq_count
                    ]

    for t in range(tiles):
        real = split(spec_ref[0, step, t * TK : (t + 1) * TK, :])
        imag = split(spec_ref[1, step, t * TK : (t + 1) * TK, :])
        left = tuple(
            jnp.concatenate(
                [jnp.concatenate([real[h], -imag[h]], axis=1), jnp.concatenate([imag[h], real[h]], axis=1)], axis=0
            )
            for h in range(2)
        )
        product = dot3(left, (w_ref[t, 0], w_ref[t, 1]))
        for c in range(2):
            out_ref[c, 0, t * TK : (t + 1) * TK, :] = product[c * TK : (c + 1) * TK, :]


def form_image(columns, weights, kx_rows):
    tiles = weights.shape[0] // kx_rows
    freq_count = weights.shape[2] // 2
    ky_count = tiles * TK
    table = radix4_tables(ky_count)
    return pl.pallas_call(
        image_kernel,
        grid=(kx_rows,),
        in_specs=[
            pl.BlockSpec(columns.shape, lambda i: (0, 0)),
            pl.BlockSpec(table.shape, lambda i: (0, 0, 0, 0)),
            pl.BlockSpec((tiles,) + weights.shape[1:], lambda i: (i, 0, 0, 0)),
        ],
        out_specs=pl.BlockSpec((2, 1, ky_count, KZ), lambda i: (0, i, 0, 0)),
        scratch_shapes=[pltpu.VMEM((2, kx_rows, ky_count, freq_count), jnp.float32)],
        out_shape=jax.ShapeDtypeStruct((2, kx_rows, ky_count, KZ), jnp.float32),
        compiler_params=pltpu.CompilerParams(vmem_limit_bytes=40 << 20),
        name="form_image",
    )(columns, jnp.asarray(table), weights)


def shards(echoes, stolt_table, kz_start, weight_ids):
    count_ax = lax.axis_size("ax")
    freqs, _, span, columns = echoes.shape
    outgoing = echoes.reshape(count_ax, freqs // count_ax, 2, span, columns)
    received = lax.all_to_all(outgoing, "ax", split_axis=0, concat_axis=0, tiled=True)
    weights = tile_weights(stolt_table, kz_start, weight_ids)
    spectrum = forward_x(received)
    everyone = ("ay", "ax", "fr")
    count = lax.axis_size(everyone)
    messages = spectrum.reshape(count, -1, columns)
    gathered = lax.all_to_all(messages, everyone, split_axis=0, concat_axis=0, tiled=True)
    return form_image(gathered.reshape(-1, columns), weights, kz_start.shape[0])


def solution(mesh):
    placed = (
        P("fr", None, "ax", "ay"),
        P(),
        P(("ay", "ax", "fr"), None),
        P(("ay", "ax", "fr"), None, None),
    )
    return jax.shard_map(
        shards,
        mesh=mesh,
        in_specs=placed,
        out_specs=P(None, ("ay", "ax", "fr"), None, None),
        check_vma=False,
    )
```

```python
import functools
import math

import jax
import jax.numpy as jnp
import ml_dtypes
import numpy as np
from jax import lax
from jax.experimental import pallas as pl
from jax.experimental.pallas import tpu as pltpu
from jax.sharding import Mesh
from jax.sharding import PartitionSpec as P

TK = 128
KZ = 384
LANES = 128


def halves_of(table):
    high = table.astype(ml_dtypes.bfloat16)
    low = (table - high.astype(np.float64)).astype(ml_dtypes.bfloat16)
    return np.stack([high, low])


def dft_table(length, scale, start=0, step=1, order=None):
    n = np.arange(length // step)
    phase = ((start + step * (n if order is None else order)[:, None]) * n[None, :]) % length
    angle = phase * (2.0 * math.pi / length)
    cosine, sine = np.cos(angle) / scale, np.sin(angle) / scale
    return halves_of(np.block([[cosine, sine], [-sine, cosine]]))


def residue_tables(length):
    return np.stack([dft_table(length, math.sqrt(length), r, 4) for r in range(4)])


def twiddles(length, radix):
    n = np.arange(length // radix)
    table = np.zeros((length // radix, LANES), np.float32)
    for r in range(radix):
        angle = (r * n % length) * (2.0 * math.pi / length)
        table[:, 2 * r], table[:, 2 * r + 1] = np.cos(angle), np.sin(angle)
    return table


def inverse_table(length):
    index = np.arange(length)
    angle = (index[:, None] * index[None, :] % length) * (2.0 * math.pi / length)
    return halves_of(np.concatenate([np.cos(angle), np.sin(angle)], axis=1) / math.sqrt(length))


def split(value):
    high = value.astype(jnp.bfloat16)
    low = (value - high.astype(jnp.float32)).astype(jnp.bfloat16)
    return high, low


def dot3(left, right, contract=((1,), (0,))):
    one = functools.partial(lax.dot_general, dimension_numbers=(contract, ((), ())), preferred_element_type=jnp.float32)
    return one(left[0], right[0]) + (one(left[1], right[0]) + one(left[0], right[1]))


def radix4(pieces):
    (ar, ai), (br, bi), (cr, ci), (dr, di) = pieces
    even = (ar + cr, ai + ci)
    odd = (br + dr, bi + di)
    even_less = (ar - cr, ai - ci)
    odd_less = (br - dr, bi - di)
    return [
        (even[0] + odd[0], even[1] + odd[1]),
        (even_less[0] + odd_less[1], even_less[1] - odd_less[0]),
        (even[0] - odd[0], even[1] - odd[1]),
        (even_less[0] - odd_less[1], even_less[1] + odd_less[0]),
    ]


def radix8(pieces):
    root = math.sqrt(0.5)
    evens, odds = radix4(pieces[0::2]), radix4(pieces[1::2])
    (ar, ai), (br, bi), (cr, ci), (dr, di) = odds
    turned = [(ar, ai), ((br + bi) * root, (bi - br) * root), (ci, -cr), ((di - dr) * root, -(dr + di) * root)]
    return [(e[0] + o[0], e[1] + o[1]) for e, o in zip(evens, turned)] + [
        (e[0] - o[0], e[1] - o[1]) for e, o in zip(evens, turned)
    ]


def weights_kernel(starts_ref, ids_ref, table_ref, inverse_ref, y_ref, out_ref, high_ref, low_ref):
    step = pl.program_id(0)
    block_count, freq_count, _ = table_ref.shape
    tiles = out_ref.shape[0]

    @pl.when(step == 0)
    def _():
        for w in range(block_count):
            high_ref[w], low_ref[w] = split(table_ref[w])

    @pl.when(step < pl.num_programs(0) - 1)
    def _():
        for t in range(tiles):
            tile = step * tiles + t
            first, second = ids_ref[2 * tile], ids_ref[2 * tile + 1]
            left = (
                jnp.concatenate([high_ref[first], high_ref[second]], axis=1),
                jnp.concatenate([low_ref[first], low_ref[second]], axis=1),
            )
            rows = pl.ds(pl.multiple_of(starts_ref[tile] * LANES, LANES), 2 * LANES)
            product = dot3(left, (inverse_ref[0, rows, :], inverse_ref[1, rows, :]))
            high, low = split(product)
            for h, half in enumerate((high, low)):
                for c in range(2):
                    out_ref[t, h, c * freq_count : (c + 1) * freq_count, :] = half[:, c * KZ : (c + 1) * KZ]

    @pl.when(step == pl.num_programs(0) - 1)
    def _():
        width = y_ref.shape[3]
        out_ref[:, :, :, :width] = y_ref[...]
        out_ref[:, :, :, width:] = jnp.zeros_like(out_ref[:, :, :, width:])


def tile_weights(stolt_table, kz_start, weight_ids):
    block_count, freq_count, block_width = stolt_table.shape
    kx_rows, tiles = kz_start.shape
    inverse = inverse_table(KZ)
    residues = residue_tables(tiles * TK)
    return pl.pallas_call(
        weights_kernel,
        grid_spec=pltpu.PrefetchScalarGridSpec(
            num_scalar_prefetch=2,
            grid=(kx_rows + 1,),
            in_specs=[
                pl.BlockSpec(stolt_table.shape, lambda i, *_: (0, 0, 0)),
                pl.BlockSpec(inverse.shape, lambda i, *_: (0, 0, 0)),
                pl.BlockSpec(residues.shape, lambda i, *_: (0, 0, 0, 0)),
            ],
            out_specs=pl.BlockSpec((tiles, 2, 2 * freq_count, KZ), lambda i, *_: (i, 0, 0, 0)),
            scratch_shapes=[pltpu.VMEM(stolt_table.shape, jnp.bfloat16)] * 2,
        ),
        out_shape=jax.ShapeDtypeStruct(((kx_rows + 1) * tiles, 2, 2 * freq_count, KZ), jnp.bfloat16),
        compiler_params=pltpu.CompilerParams(vmem_limit_bytes=24 << 20),
        name="tile_weights",
    )(kz_start.reshape(-1), weight_ids.reshape(-1), stolt_table, jnp.asarray(inverse), jnp.asarray(residues))


def forward_x_kernel(x_ref, twiddle_ref, table_ref, out_ref):
    sources, freqs, _, span, _ = x_ref.shape
    per = sources // 8
    piece = per * span
    pieces = []
    for q in range(8):
        pieces.append(
            tuple(
                jnp.concatenate([x_ref[q * per : (q + 1) * per, f, c].reshape(piece, LANES) for f in range(freqs)], axis=1)
                for c in range(2)
            )
        )
    table = (table_ref[0], table_ref[1])
    message = 4 * freqs * 2
    run = piece // 2
    for r, (real, imag) in enumerate(radix8(pieces)):
        if r > 0:
            cosine, sine = twiddle_ref[:, 2 * r : 2 * r + 1], twiddle_ref[:, 2 * r + 1 : 2 * r + 2]
            real, imag = real * cosine + imag * sine, imag * cosine - real * sine
        product = dot3(table, split(jnp.concatenate([real, imag], axis=0)))
        z_hi, row = r // 4, r % 4
        for c in range(2):
            for core in range(2):
                rows = slice(c * piece + core * run, c * piece + (core + 1) * run)
                for f in range(freqs):
                    at = (core * 2 + z_hi) * run * message + (c * 4 + row) * freqs + f
                    out_ref[pl.ds(at, run, stride=message), :] = product[rows, f * LANES : (f + 1) * LANES]


def forward_x(received, order):
    sources, freqs, _, span, columns = received.shape
    length = sources * span
    twiddle = twiddles(length, 8)
    table = dft_table(length // 8, math.sqrt(length), order=order)
    return pl.pallas_call(
        forward_x_kernel,
        out_shape=jax.ShapeDtypeStruct((length * freqs * 2, columns), jnp.float32),
        compiler_params=pltpu.CompilerParams(vmem_limit_bytes=24 << 20),
        name="forward_x",
    )(received, jnp.asarray(twiddle), jnp.asarray(table))


def image_kernel(s_ref, w_ref, out_ref, spec_ref, stage_ref, out_sems):
    _, kx_rows, ky_count, freq_count = spec_ref.shape
    tiles = ky_count // TK
    message = 4 * kx_rows
    y_tables = w_ref.shape[0] - 4
    y_width = ky_count // 2
    sources = s_ref.shape[0] // (4 * message)
    whole = s_ref[...].reshape(sources, 4, 2, message // 2, LANES)
    turned = [[jnp.swapaxes(whole[:, q, c], 0, 1) for c in range(2)] for q in range(4)]
    for pair in range(0, kx_rows, 2):
        halves = [[] for _ in range(4)]
        for r in range(pair, pair + 2):
            pieces = []
            for q in range(4):
                parts = []
                for c in range(2):
                    rows = turned[q][c]
                    parts.append(jnp.concatenate([rows[r * 2], rows[r * 2 + 1]], axis=0))
                pieces.append(tuple(parts))
            for residue, (real, imag) in enumerate(radix4(pieces)):
                halves[residue].append(split(jnp.concatenate([real, imag], axis=1)))
        for residue in range(4):
            right = tuple(jnp.concatenate([pair_of[h] for pair_of in halves[residue]], axis=0) for h in range(2))
            table = tuple(w_ref[y_tables + residue, h, :, :y_width] for h in range(2))
            product = dot3(table, right, ((1,), (1,)))
            for c in range(2):
                for j in range(2):
                    spec_ref[c, pair + j, pl.ds(residue, ky_count // 4, stride=4), :] = product[
                        c * ky_count // 4 : (c + 1) * ky_count // 4, j * freq_count : (j + 1) * freq_count
                    ]

    copies = []
    for r in range(kx_rows):
        for t in range(tiles):
            rows = slice(t * TK, (t + 1) * TK)
            real = split(spec_ref[0, r, rows, :])
            imag = split(spec_ref[1, r, rows, :])
            left = tuple(jnp.concatenate([real[h], imag[h]], axis=1) for h in range(2))
            tile = r * tiles + t
            right = tuple(
                jnp.concatenate(
                    [
                        jnp.concatenate([w_ref[tile, h, :freq_count], w_ref[tile, h, freq_count:]], axis=1),
                        jnp.concatenate([-w_ref[tile, h, freq_count:], w_ref[tile, h, :freq_count]], axis=1),
                    ],
                    axis=0,
                )
                for h in range(2)
            )
            product = dot3(left, right)
            for c in range(2):
                stage_ref[c, r, rows, :] = product[:, c * KZ : (c + 1) * KZ]
            at = (slice(None), r, pl.ds(t * TK, TK), slice(None))
            copies.append(pltpu.make_async_copy(stage_ref.at[at], out_ref.at[at], out_sems.at[tile]))
            copies[-1].start()
    for copy in copies:
        copy.wait()


def form_image(columns, weights, kx_rows):
    tiles = weights.shape[0] // (kx_rows + 1)
    freq_count = weights.shape[2] // 2
    ky_count = tiles * TK
    shape = (2, kx_rows, ky_count, KZ)
    return pl.pallas_call(
        image_kernel,
        out_specs=pl.BlockSpec(memory_space=pltpu.HBM),
        scratch_shapes=[
            pltpu.VMEM((2, kx_rows, ky_count, freq_count), jnp.float32),
            pltpu.VMEM(shape, jnp.float32),
            pltpu.SemaphoreType.DMA((kx_rows * tiles,)),
        ],
        out_shape=jax.ShapeDtypeStruct(shape, jnp.float32),
        compiler_params=pltpu.CompilerParams(vmem_limit_bytes=28 << 20),
        name="form_image",
    )(columns, weights)


EVERYONE = ("core", "z_hi", "z_lo", "y", "x")


def exchange_order(sizes):
    place = ("x", "y", "z_lo", "core")
    blocks = np.arange(math.prod(sizes[a] for a in place)).reshape([sizes[a] for a in place])
    return blocks.transpose([place.index(a) for a in EVERYONE if a in place]).reshape(-1)


def shards(echoes, stolt_table, kz_start, weight_ids):
    sizes = {a: lax.axis_size(a) for a in EVERYONE}
    ax = ("y", "z_lo", "core")
    count_ax = math.prod(sizes[a] for a in ax)
    freqs, _, span, columns = echoes.shape
    share = freqs // count_ax
    outgoing = echoes.reshape(count_ax, share, 2, span, columns)
    received = lax.all_to_all(outgoing, ax, split_axis=0, concat_axis=0, tiled=True)

    blocks, freq_count, width = stolt_table.shape
    split_table = stolt_table.reshape(blocks, sizes["z_hi"], sizes["y"], sizes["z_lo"], sizes["core"], share, width)
    ordered = split_table.transpose(0, 5, 4, 1, 3, 2, 6).reshape(blocks, freq_count, width)
    weights = tile_weights(ordered, kz_start, weight_ids)

    spectrum = forward_x(received, exchange_order(sizes))
    spectrum, weights = lax.optimization_barrier((spectrum, weights))
    count = math.prod(sizes.values())
    messages = spectrum.reshape(count, -1, columns)
    gathered = lax.all_to_all(messages, EVERYONE, split_axis=0, concat_axis=0, tiled=True)
    return form_image(gathered.reshape(-1, columns), weights, kz_start.shape[0])


def solution(mesh):
    y, z_lo, core = 4, 4, 2
    fine = Mesh(
        mesh.devices.reshape(y, z_lo, core, mesh.shape["ay"], mesh.shape["fr"]), ("y", "z_lo", "core", "x", "z_hi")
    )
    kx = ("x", "y", "z_lo", "core", "z_hi")
    placed = (
        P("z_hi", None, ("y", "z_lo", "core"), "x"),
        P(),
        P(kx, None),
        P(kx, None, None),
    )
    return jax.shard_map(
        shards,
        mesh=fine,
        in_specs=placed,
        out_specs=P(None, kx, None, None),
        check_vma=False,
    )
```

```python
import functools
import math

import jax
import jax.numpy as jnp
import ml_dtypes
import numpy as np
from jax import lax
from jax.experimental import pallas as pl
from jax.experimental.pallas import tpu as pltpu
from jax.sharding import Mesh
from jax.sharding import PartitionSpec as P

TK = 128
KZ = 384
LANES = 128


def halves_of(table):
    high = table.astype(ml_dtypes.bfloat16)
    low = (table - high.astype(np.float64)).astype(ml_dtypes.bfloat16)
    return np.stack([high, low])


def dft_table(length, scale, start=0, step=1):
    n = np.arange(length // step)
    phase = ((start + step * n[:, None]) * n[None, :]) % length
    angle = phase * (2.0 * math.pi / length)
    cosine, sine = np.cos(angle) / scale, np.sin(angle) / scale
    return halves_of(np.block([[cosine, sine], [-sine, cosine]]))


def residue_tables(length):
    return np.stack([dft_table(length, math.sqrt(length), r, 4) for r in range(4)])


def turn(phase, length):
    shifted = (phase & (length - 1)) + length // 8
    quadrant = (shifted >> ((length // 4).bit_length() - 1)) & 3
    angle = ((shifted & (length // 4 - 1)) - length // 8).astype(jnp.float32) * (2.0 * math.pi / length)
    square = angle * angle
    sine = 1.0 / 362880
    for term in (-1.0 / 5040, 1.0 / 120, -1.0 / 6, 1.0):
        sine = sine * square + term
    sine = sine * angle
    cosine = 1.0 / 40320
    for term in (-1.0 / 720, 1.0 / 24, -0.5, 1.0):
        cosine = cosine * square + term
    swapped = (quadrant & 1) == 1
    first = jnp.where(swapped, sine, cosine)
    second = jnp.where(swapped, cosine, sine)
    first = jnp.where(((quadrant + 1) & 2) == 2, -first, first)
    second = jnp.where((quadrant & 2) == 2, -second, second)
    return first, second


def inverse_table(length):
    index = np.arange(length)
    angle = (index[:, None] * index[None, :] % length) * (2.0 * math.pi / length)
    return halves_of(np.concatenate([np.cos(angle), np.sin(angle)], axis=1) / math.sqrt(length))


def split(value):
    high = value.astype(jnp.bfloat16)
    low = (value - high.astype(jnp.float32)).astype(jnp.bfloat16)
    return high, low


def dot3(left, right, contract=((1,), (0,))):
    one = functools.partial(lax.dot_general, dimension_numbers=(contract, ((), ())), preferred_element_type=jnp.float32)
    return one(left[0], right[0]) + (one(left[1], right[0]) + one(left[0], right[1]))


def radix4(pieces):
    (ar, ai), (br, bi), (cr, ci), (dr, di) = pieces
    even = (ar + cr, ai + ci)
    odd = (br + dr, bi + di)
    even_less = (ar - cr, ai - ci)
    odd_less = (br - dr, bi - di)
    return [
        (even[0] + odd[0], even[1] + odd[1]),
        (even_less[0] + odd_less[1], even_less[1] - odd_less[0]),
        (even[0] - odd[0], even[1] - odd[1]),
        (even_less[0] - odd_less[1], even_less[1] + odd_less[0]),
    ]


def radix8(pieces):
    root = math.sqrt(0.5)
    evens, odds = radix4(pieces[0::2]), radix4(pieces[1::2])
    (ar, ai), (br, bi), (cr, ci), (dr, di) = odds
    turned = [(ar, ai), ((br + bi) * root, (bi - br) * root), (ci, -cr), ((di - dr) * root, -(dr + di) * root)]
    return [(e[0] + o[0], e[1] + o[1]) for e, o in zip(evens, turned)] + [
        (e[0] - o[0], e[1] - o[1]) for e, o in zip(evens, turned)
    ]


def weights_kernel(starts_ref, ids_ref, table_ref, inverse_ref, y_ref, out_ref, high_ref, low_ref):
    step = pl.program_id(0)
    block_count, freq_count, _ = table_ref.shape
    tiles = out_ref.shape[0]

    @pl.when(step == 0)
    def _():
        for w in range(block_count):
            high_ref[w], low_ref[w] = split(table_ref[w])

    @pl.when(step < pl.num_programs(0) - 1)
    def _():
        for t in range(tiles):
            tile = step * tiles + t
            first, second = ids_ref[2 * tile], ids_ref[2 * tile + 1]
            left = (
                jnp.concatenate([high_ref[first], high_ref[second]], axis=1),
                jnp.concatenate([low_ref[first], low_ref[second]], axis=1),
            )
            rows = pl.ds(pl.multiple_of(starts_ref[tile] * LANES, LANES), 2 * LANES)
            product = dot3(left, (inverse_ref[0, rows, :], inverse_ref[1, rows, :]))
            high, low = split(product)
            for h, half in enumerate((high, low)):
                for c in range(2):
                    out_ref[t, h, c * freq_count : (c + 1) * freq_count, :] = half[:, c * KZ : (c + 1) * KZ]

    @pl.when(step == pl.num_programs(0) - 1)
    def _():
        width = y_ref.shape[3]
        out_ref[:, :, :, :width] = y_ref[...]
        out_ref[:, :, :, width:] = jnp.zeros_like(out_ref[:, :, :, width:])


def tile_weights(stolt_table, kz_start, weight_ids):
    block_count, freq_count, block_width = stolt_table.shape
    kx_rows, tiles = kz_start.shape
    inverse = inverse_table(KZ)
    residues = residue_tables(tiles * TK)
    return pl.pallas_call(
        weights_kernel,
        grid_spec=pltpu.PrefetchScalarGridSpec(
            num_scalar_prefetch=2,
            grid=(kx_rows + 1,),
            in_specs=[
                pl.BlockSpec(stolt_table.shape, lambda i, *_: (0, 0, 0)),
                pl.BlockSpec(inverse.shape, lambda i, *_: (0, 0, 0)),
                pl.BlockSpec(residues.shape, lambda i, *_: (0, 0, 0, 0)),
            ],
            out_specs=pl.BlockSpec((tiles, 2, 2 * freq_count, KZ), lambda i, *_: (i, 0, 0, 0)),
            scratch_shapes=[pltpu.VMEM(stolt_table.shape, jnp.bfloat16)] * 2,
        ),
        out_shape=jax.ShapeDtypeStruct(((kx_rows + 1) * tiles, 2, 2 * freq_count, KZ), jnp.bfloat16),
        compiler_params=pltpu.CompilerParams(vmem_limit_bytes=24 << 20),
        name="tile_weights",
    )(kz_start.reshape(-1), weight_ids.reshape(-1), stolt_table, jnp.asarray(inverse), jnp.asarray(residues))


def forward_x_kernel(order, x_ref, out_ref):
    sources, freqs, _, span, _ = x_ref.shape
    per = sources // 8
    piece = per * span
    pieces = []
    for q in range(8):
        pieces.append(
            tuple(
                jnp.concatenate([x_ref[q * per : (q + 1) * per, f, c].reshape(piece, LANES) for f in range(freqs)], axis=1)
                for c in range(2)
            )
        )
    row = lax.broadcasted_iota(jnp.int32, (piece, piece), 0)
    n = lax.broadcasted_iota(jnp.int32, (piece, piece), 1)
    k = sum(((row >> shift) & (size - 1)) * stride for shift, size, stride in order)
    cosine, sine = turn(k * n, piece)
    scale = 1.0 / math.sqrt(8 * piece)
    (cos_high, cos_low), (sin_high, sin_low) = split(cosine * scale), split(sine * scale)
    table = tuple(
        jnp.concatenate([jnp.concatenate([c, s], axis=1), jnp.concatenate([-s, c], axis=1)], axis=0)
        for c, s in ((cos_high, sin_high), (cos_low, sin_low))
    )
    column = lax.broadcasted_iota(jnp.int32, (piece, LANES), 1)
    cosines, sines = turn(lax.broadcasted_iota(jnp.int32, (piece, LANES), 0) * column, 8 * piece)
    message = 4 * freqs * 2
    run = piece // 2
    for r, (real, imag) in enumerate(radix8(pieces)):
        if r > 0:
            cosine, sine = cosines[:, r : r + 1], sines[:, r : r + 1]
            real, imag = real * cosine + imag * sine, imag * cosine - real * sine
        product = dot3(table, split(jnp.concatenate([real, imag], axis=0)))
        z_hi, row = r // 4, r % 4
        for c in range(2):
            for core in range(2):
                rows = slice(c * piece + core * run, c * piece + (core + 1) * run)
                for f in range(freqs):
                    at = (core * 2 + z_hi) * run * message + (c * 4 + row) * freqs + f
                    out_ref[pl.ds(at, run, stride=message), :] = product[rows, f * LANES : (f + 1) * LANES]


def forward_x(received, order):
    sources, freqs, _, span, columns = received.shape
    return pl.pallas_call(
        functools.partial(forward_x_kernel, order),
        out_shape=jax.ShapeDtypeStruct((sources * span * freqs * 2, columns), jnp.float32),
        compiler_params=pltpu.CompilerParams(vmem_limit_bytes=24 << 20),
        name="forward_x",
    )(received)


def image_kernel(s_ref, w_ref, out_ref, spec_ref, stage_ref, out_sems):
    _, kx_rows, ky_count, freq_count = spec_ref.shape
    tiles = ky_count // TK
    message = 4 * kx_rows
    y_tables = w_ref.shape[0] - 4
    y_width = ky_count // 2
    sources = s_ref.shape[0] // (4 * message)
    whole = s_ref[...].reshape(sources, 4, 2, message // 2, LANES)
    turned = [[jnp.swapaxes(whole[:, q, c], 0, 1) for c in range(2)] for q in range(4)]
    for pair in range(0, kx_rows, 2):
        halves = [[] for _ in range(4)]
        for r in range(pair, pair + 2):
            pieces = []
            for q in range(4):
                parts = []
                for c in range(2):
                    rows = turned[q][c]
                    parts.append(jnp.concatenate([rows[r * 2], rows[r * 2 + 1]], axis=0))
                pieces.append(tuple(parts))
            for residue, (real, imag) in enumerate(radix4(pieces)):
                halves[residue].append(split(jnp.concatenate([real, imag], axis=1)))
        for residue in range(4):
            right = tuple(jnp.concatenate([pair_of[h] for pair_of in halves[residue]], axis=0) for h in range(2))
            table = tuple(w_ref[y_tables + residue, h, :, :y_width] for h in range(2))
            product = dot3(table, right, ((1,), (1,)))
            for c in range(2):
                for j in range(2):
                    spec_ref[c, pair + j, pl.ds(residue, ky_count // 4, stride=4), :] = product[
                        c * ky_count // 4 : (c + 1) * ky_count // 4, j * freq_count : (j + 1) * freq_count
                    ]

    copies = []
    for r in range(kx_rows):
        for t in range(tiles):
            rows = slice(t * TK, (t + 1) * TK)
            real = split(spec_ref[0, r, rows, :])
            imag = split(spec_ref[1, r, rows, :])
            left = tuple(jnp.concatenate([real[h], imag[h]], axis=1) for h in range(2))
            tile = r * tiles + t
            right = tuple(
                jnp.concatenate(
                    [
                        jnp.concatenate([w_ref[tile, h, :freq_count], w_ref[tile, h, freq_count:]], axis=1),
                        jnp.concatenate([-w_ref[tile, h, freq_count:], w_ref[tile, h, :freq_count]], axis=1),
                    ],
                    axis=0,
                )
                for h in range(2)
            )
            product = dot3(left, right)
            for c in range(2):
                stage_ref[c, r, rows, :] = product[:, c * KZ : (c + 1) * KZ]
            at = (slice(None), r, pl.ds(t * TK, TK), slice(None))
            copies.append(pltpu.make_async_copy(stage_ref.at[at], out_ref.at[at], out_sems.at[tile]))
            copies[-1].start()
    for copy in copies:
        copy.wait()


def form_image(columns, weights, kx_rows):
    tiles = weights.shape[0] // (kx_rows + 1)
    freq_count = weights.shape[2] // 2
    ky_count = tiles * TK
    shape = (2, kx_rows, ky_count, KZ)
    return pl.pallas_call(
        image_kernel,
        out_specs=pl.BlockSpec(memory_space=pltpu.HBM),
        scratch_shapes=[
            pltpu.VMEM((2, kx_rows, ky_count, freq_count), jnp.float32),
            pltpu.VMEM(shape, jnp.float32),
            pltpu.SemaphoreType.DMA((kx_rows * tiles,)),
        ],
        out_shape=jax.ShapeDtypeStruct(shape, jnp.float32),
        compiler_params=pltpu.CompilerParams(vmem_limit_bytes=28 << 20),
        name="form_image",
    )(columns, weights)


EVERYONE = ("core", "z_hi", "z_lo", "y", "x")


def exchange_order(sizes):
    strides, shifts = {}, {}
    for places, axes in ((strides, ("x", "y", "z_lo", "core")), (shifts, [a for a in EVERYONE if a != "z_hi"])):
        stride = 1
        for axis in reversed(axes):
            places[axis] = stride
            stride *= sizes[axis]
    return [(shifts[a].bit_length() - 1, sizes[a], strides[a]) for a in strides]


def shards(echoes, stolt_table, kz_start, weight_ids):
    sizes = {a: lax.axis_size(a) for a in EVERYONE}
    ax = ("y", "z_lo", "core")
    count_ax = math.prod(sizes[a] for a in ax)
    freqs, _, span, columns = echoes.shape
    share = freqs // count_ax
    outgoing = echoes.reshape(count_ax, share, 2, span, columns)
    received = lax.all_to_all(outgoing, ax, split_axis=0, concat_axis=0, tiled=True)

    blocks, freq_count, width = stolt_table.shape
    split_table = stolt_table.reshape(blocks, sizes["z_hi"], sizes["y"], sizes["z_lo"], sizes["core"], share, width)
    ordered = split_table.transpose(0, 5, 4, 1, 3, 2, 6).reshape(blocks, freq_count, width)
    weights = tile_weights(ordered, kz_start, weight_ids)

    spectrum = forward_x(received, exchange_order(sizes))
    spectrum, weights = lax.optimization_barrier((spectrum, weights))
    count = math.prod(sizes.values())
    messages = spectrum.reshape(count, -1, columns)
    gathered = lax.all_to_all(messages, EVERYONE, split_axis=0, concat_axis=0, tiled=True)
    return form_image(gathered.reshape(-1, columns), weights, kz_start.shape[0])


def solution(mesh):
    y, z_lo, core = 4, 4, 2
    fine = Mesh(
        mesh.devices.reshape(y, z_lo, core, mesh.shape["ay"], mesh.shape["fr"]), ("y", "z_lo", "core", "x", "z_hi")
    )
    kx = ("x", "y", "z_lo", "core", "z_hi")
    placed = (
        P("z_hi", None, ("y", "z_lo", "core"), "x"),
        P(),
        P(kx, None),
        P(kx, None, None),
    )
    return jax.shard_map(
        shards,
        mesh=fine,
        in_specs=placed,
        out_specs=P(None, kx, None, None),
        check_vma=False,
    )
```

```python
import functools
import math

import jax
import jax.numpy as jnp
import ml_dtypes
import numpy as np
from jax import lax
from jax.experimental import pallas as pl
from jax.experimental.pallas import tpu as pltpu
from jax.sharding import Mesh
from jax.sharding import PartitionSpec as P

TK = 128
KZ = 384
LANES = 128


def halves_of(table):
    high = table.astype(ml_dtypes.bfloat16)
    low = (table - high.astype(np.float64)).astype(ml_dtypes.bfloat16)
    return np.stack([high, low])


def dft_table(length, scale, start=0, step=1):
    n = np.arange(length // step)
    phase = ((start + step * n[:, None]) * n[None, :]) % length
    angle = phase * (2.0 * math.pi / length)
    cosine, sine = np.cos(angle) / scale, np.sin(angle) / scale
    return halves_of(np.block([[cosine, sine], [-sine, cosine]]))


def residue_tables(length):
    return np.stack([dft_table(length, math.sqrt(length), r, 4) for r in range(4)])


def turn(phase, length):
    shifted = (phase & (length - 1)) + length // 8
    quadrant = (shifted >> ((length // 4).bit_length() - 1)) & 3
    angle = ((shifted & (length // 4 - 1)) - length // 8).astype(jnp.float32) * (2.0 * math.pi / length)
    square = angle * angle
    sine = 1.0 / 362880
    for term in (-1.0 / 5040, 1.0 / 120, -1.0 / 6, 1.0):
        sine = sine * square + term
    sine = sine * angle
    cosine = 1.0 / 40320
    for term in (-1.0 / 720, 1.0 / 24, -0.5, 1.0):
        cosine = cosine * square + term
    swapped = (quadrant & 1) == 1
    first = jnp.where(swapped, sine, cosine)
    second = jnp.where(swapped, cosine, sine)
    first = jnp.where(((quadrant + 1) & 2) == 2, -first, first)
    second = jnp.where((quadrant & 2) == 2, -second, second)
    return first, second


def inverse_table(length):
    index = np.arange(length)
    angle = (index[:, None] * index[None, :] % length) * (2.0 * math.pi / length)
    return halves_of(np.concatenate([np.cos(angle), np.sin(angle)], axis=1) / math.sqrt(length))


def split(value):
    high = value.astype(jnp.bfloat16)
    low = (value - high.astype(jnp.float32)).astype(jnp.bfloat16)
    return high, low


def dot3(left, right, contract=((1,), (0,))):
    one = functools.partial(lax.dot_general, dimension_numbers=(contract, ((), ())), preferred_element_type=jnp.float32)
    return one(left[0], right[0]) + (one(left[1], right[0]) + one(left[0], right[1]))


def radix4(pieces):
    (ar, ai), (br, bi), (cr, ci), (dr, di) = pieces
    even = (ar + cr, ai + ci)
    odd = (br + dr, bi + di)
    even_less = (ar - cr, ai - ci)
    odd_less = (br - dr, bi - di)
    return [
        (even[0] + odd[0], even[1] + odd[1]),
        (even_less[0] + odd_less[1], even_less[1] - odd_less[0]),
        (even[0] - odd[0], even[1] - odd[1]),
        (even_less[0] - odd_less[1], even_less[1] + odd_less[0]),
    ]


def radix8(pieces):
    root = math.sqrt(0.5)
    evens, odds = radix4(pieces[0::2]), radix4(pieces[1::2])
    (ar, ai), (br, bi), (cr, ci), (dr, di) = odds
    turned = [(ar, ai), ((br + bi) * root, (bi - br) * root), (ci, -cr), ((di - dr) * root, -(dr + di) * root)]
    return [(e[0] + o[0], e[1] + o[1]) for e, o in zip(evens, turned)] + [
        (e[0] - o[0], e[1] - o[1]) for e, o in zip(evens, turned)
    ]


def weights_kernel(starts_ref, ids_ref, table_ref, inverse_ref, y_ref, out_ref, high_ref, low_ref):
    step = pl.program_id(0)
    block_count, freq_count, _ = table_ref.shape
    tiles = out_ref.shape[0]

    @pl.when(step == 0)
    def _():
        for w in range(block_count):
            high_ref[w], low_ref[w] = split(table_ref[w])

    @pl.when(step < pl.num_programs(0) - 1)
    def _():
        for t in range(tiles):
            tile = step * tiles + t
            first, second = ids_ref[2 * tile], ids_ref[2 * tile + 1]
            left = (
                jnp.concatenate([high_ref[first], high_ref[second]], axis=1),
                jnp.concatenate([low_ref[first], low_ref[second]], axis=1),
            )
            rows = pl.ds(pl.multiple_of(starts_ref[tile] * LANES, LANES), 2 * LANES)
            product = dot3(left, (inverse_ref[0, rows, :], inverse_ref[1, rows, :]))
            high, low = split(product)
            for h, half in enumerate((high, low)):
                for c in range(2):
                    out_ref[t, h, c * freq_count : (c + 1) * freq_count, :] = half[:, c * KZ : (c + 1) * KZ]

    @pl.when(step == pl.num_programs(0) - 1)
    def _():
        width = y_ref.shape[3]
        out_ref[:, :, :, :width] = y_ref[...]
        out_ref[:, :, :, width:] = jnp.zeros_like(out_ref[:, :, :, width:])


def tile_weights(stolt_table, kz_start, weight_ids):
    block_count, freq_count, block_width = stolt_table.shape
    kx_rows, tiles = kz_start.shape
    inverse = inverse_table(KZ)
    residues = residue_tables(tiles * TK)
    return pl.pallas_call(
        weights_kernel,
        grid_spec=pltpu.PrefetchScalarGridSpec(
            num_scalar_prefetch=2,
            grid=(kx_rows + 1,),
            in_specs=[
                pl.BlockSpec(stolt_table.shape, lambda i, *_: (0, 0, 0)),
                pl.BlockSpec(inverse.shape, lambda i, *_: (0, 0, 0)),
                pl.BlockSpec(residues.shape, lambda i, *_: (0, 0, 0, 0)),
            ],
            out_specs=pl.BlockSpec((tiles, 2, 2 * freq_count, KZ), lambda i, *_: (i, 0, 0, 0)),
            scratch_shapes=[pltpu.VMEM(stolt_table.shape, jnp.bfloat16)] * 2,
        ),
        out_shape=jax.ShapeDtypeStruct(((kx_rows + 1) * tiles, 2, 2 * freq_count, KZ), jnp.bfloat16),
        compiler_params=pltpu.CompilerParams(vmem_limit_bytes=24 << 20),
        name="tile_weights",
    )(kz_start.reshape(-1), weight_ids.reshape(-1), stolt_table, jnp.asarray(inverse), jnp.asarray(residues))


def forward_x_kernel(order, slots, x_ref, out_ref):
    sources, freqs, _, span, _ = x_ref.shape
    per = sources // 8
    piece = per * span
    pieces = []
    for q in range(8):
        pieces.append(
            tuple(
                jnp.concatenate(
                    [jnp.concatenate([x_ref[slot, f, c] for slot in slots[q * per : (q + 1) * per]], axis=0) for f in range(freqs)],
                    axis=1,
                )
                for c in range(2)
            )
        )
    row = lax.broadcasted_iota(jnp.int32, (piece, piece), 0)
    n = lax.broadcasted_iota(jnp.int32, (piece, piece), 1)
    k = sum(((row >> shift) & (size - 1)) * stride for shift, size, stride in order)
    cosine, sine = turn(k * n, piece)
    scale = 1.0 / math.sqrt(8 * piece)
    (cos_high, cos_low), (sin_high, sin_low) = split(cosine * scale), split(sine * scale)
    table = tuple(
        jnp.concatenate([jnp.concatenate([c, s], axis=1), jnp.concatenate([-s, c], axis=1)], axis=0)
        for c, s in ((cos_high, sin_high), (cos_low, sin_low))
    )
    column = lax.broadcasted_iota(jnp.int32, (piece, LANES), 1)
    cosines, sines = turn(lax.broadcasted_iota(jnp.int32, (piece, LANES), 0) * column, 8 * piece)
    message = 4 * freqs * 2
    for r, (real, imag) in enumerate(radix8(pieces)):
        if r > 0:
            cosine, sine = cosines[:, r : r + 1], sines[:, r : r + 1]
            real, imag = real * cosine + imag * sine, imag * cosine - real * sine
        product = dot3(table, split(jnp.concatenate([real, imag], axis=0)))
        z_hi, row = r // 4, r % 4
        for c in range(2):
            for f in range(freqs):
                at = z_hi * message + (c * 4 + row) * freqs + f
                out_ref[pl.ds(at, piece, stride=2 * message), :] = product[
                    c * piece : (c + 1) * piece, f * LANES : (f + 1) * LANES
                ]


def forward_x(received, order, slots):
    sources, freqs, _, span, columns = received.shape
    return pl.pallas_call(
        functools.partial(forward_x_kernel, order, slots),
        out_shape=jax.ShapeDtypeStruct((sources * span * freqs * 2, columns), jnp.float32),
        compiler_params=pltpu.CompilerParams(vmem_limit_bytes=24 << 20),
        name="forward_x",
    )(received)


def image_kernel(before, s_ref, w_ref, out_ref, spec_ref, stage_ref, out_sems):
    _, kx_rows, ky_count, freq_count = spec_ref.shape
    tiles = ky_count // TK
    message = 4 * kx_rows
    y_tables = w_ref.shape[0] - 4
    y_width = ky_count // 2
    sources = s_ref.shape[0] // (4 * message)
    whole = s_ref[...].reshape(before, 4, sources // before, 2, message // 2, LANES)
    turned = [
        [jnp.swapaxes(whole[:, q, :, c].reshape(sources, message // 2, LANES), 0, 1) for c in range(2)] for q in range(4)
    ]
    for pair in range(0, kx_rows, 2):
        halves = [[] for _ in range(4)]
        for r in range(pair, pair + 2):
            pieces = []
            for q in range(4):
                parts = []
                for c in range(2):
                    rows = turned[q][c]
                    parts.append(jnp.concatenate([rows[r * 2], rows[r * 2 + 1]], axis=0))
                pieces.append(tuple(parts))
            for residue, (real, imag) in enumerate(radix4(pieces)):
                halves[residue].append(split(jnp.concatenate([real, imag], axis=1)))
        for residue in range(4):
            right = tuple(jnp.concatenate([pair_of[h] for pair_of in halves[residue]], axis=0) for h in range(2))
            table = tuple(w_ref[y_tables + residue, h, :, :y_width] for h in range(2))
            product = dot3(table, right, ((1,), (1,)))
            for c in range(2):
                for j in range(2):
                    spec_ref[c, pair + j, pl.ds(residue, ky_count // 4, stride=4), :] = product[
                        c * ky_count // 4 : (c + 1) * ky_count // 4, j * freq_count : (j + 1) * freq_count
                    ]

    copies = []
    for r in range(kx_rows):
        for t in range(tiles):
            rows = slice(t * TK, (t + 1) * TK)
            real = split(spec_ref[0, r, rows, :])
            imag = split(spec_ref[1, r, rows, :])
            left = tuple(jnp.concatenate([real[h], imag[h]], axis=1) for h in range(2))
            tile = r * tiles + t
            right = tuple(
                jnp.concatenate(
                    [
                        jnp.concatenate([w_ref[tile, h, :freq_count], w_ref[tile, h, freq_count:]], axis=1),
                        jnp.concatenate([-w_ref[tile, h, freq_count:], w_ref[tile, h, :freq_count]], axis=1),
                    ],
                    axis=0,
                )
                for h in range(2)
            )
            product = dot3(left, right)
            for c in range(2):
                stage_ref[c, r, rows, :] = product[:, c * KZ : (c + 1) * KZ]
            at = (slice(None), r, pl.ds(t * TK, TK), slice(None))
            copies.append(pltpu.make_async_copy(stage_ref.at[at], out_ref.at[at], out_sems.at[tile]))
            copies[-1].start()
    for copy in copies:
        copy.wait()


def form_image(columns, weights, kx_rows, before):
    tiles = weights.shape[0] // (kx_rows + 1)
    freq_count = weights.shape[2] // 2
    ky_count = tiles * TK
    shape = (2, kx_rows, ky_count, KZ)
    return pl.pallas_call(
        functools.partial(image_kernel, before),
        out_specs=pl.BlockSpec(memory_space=pltpu.HBM),
        scratch_shapes=[
            pltpu.VMEM((2, kx_rows, ky_count, freq_count), jnp.float32),
            pltpu.VMEM(shape, jnp.float32),
            pltpu.SemaphoreType.DMA((kx_rows * tiles,)),
        ],
        out_shape=jax.ShapeDtypeStruct(shape, jnp.float32),
        compiler_params=pltpu.CompilerParams(vmem_limit_bytes=28 << 20),
        name="form_image",
    )(columns, weights)


APERTURE_X = ("y", "z_lo", "core")
KX = ("x", "y", "z_lo", "core", "z_hi")
FIRST = ("y", "core", "z_lo")
SECOND = ("core", "y", "z_lo", "x", "z_hi")


def strides(axes, sizes):
    result, stride = {}, 1
    for axis in reversed(axes):
        result[axis] = stride
        stride *= sizes[axis]
    return result


def product_of(axes, sizes):
    return math.prod(sizes[axis] for axis in axes)


def shards(echoes, stolt_table, kz_start, weight_ids):
    sizes = {axis: lax.axis_size(axis) for axis in KX}
    count_ax = product_of(FIRST, sizes)
    freqs, _, span, columns = echoes.shape
    share = freqs // count_ax
    outgoing = echoes.reshape(count_ax, share, 2, span, columns)
    received = lax.all_to_all(outgoing, FIRST, split_axis=0, concat_axis=0, tiled=True)

    blocks, freq_count, width = stolt_table.shape
    held = ("z_hi",) + FIRST
    arriving = [axis for axis in SECOND if axis != "x"]
    ordered = stolt_table.reshape((blocks,) + tuple(sizes[axis] for axis in held) + (share, width))
    ordered = ordered.transpose([0, len(held) + 1] + [1 + held.index(axis) for axis in arriving] + [len(held) + 2])
    weights = tile_weights(ordered.reshape(blocks, freq_count, width), kz_start, weight_ids)

    in_slot = strides(FIRST, sizes)
    grid = np.indices([sizes[axis] for axis in APERTURE_X]).reshape(len(APERTURE_X), -1)
    slots = [int(slot) for slot in sum(grid[i] * in_slot[axis] for i, axis in enumerate(APERTURE_X))]
    in_row, in_kx = strides(SECOND[:-1], sizes), strides(KX[:-1], sizes)
    order = [(in_row[axis].bit_length() - 1, sizes[axis], in_kx[axis]) for axis in in_kx]
    spectrum = forward_x(received, order, slots)
    spectrum, weights = lax.optimization_barrier((spectrum, weights))
    messages = spectrum.reshape(product_of(SECOND, sizes), -1, columns)
    gathered = lax.all_to_all(messages, SECOND, split_axis=0, concat_axis=0, tiled=True)
    before = product_of(SECOND[: SECOND.index("x")], sizes)
    return form_image(gathered.reshape(-1, columns), weights, kz_start.shape[0], before)


def solution(mesh):
    y, z_lo, core = 4, 4, 2
    fine = Mesh(
        mesh.devices.reshape(y, z_lo, core, mesh.shape["ay"], mesh.shape["fr"]), ("y", "z_lo", "core", "x", "z_hi")
    )
    placed = (
        P("z_hi", None, APERTURE_X, "x"),
        P(),
        P(KX, None),
        P(KX, None, None),
    )
    return jax.shard_map(
        shards,
        mesh=fine,
        in_specs=placed,
        out_specs=P(None, KX, None, None),
        check_vma=False,
    )
```

```python
import functools
import math

import jax
import jax.numpy as jnp
import ml_dtypes
import numpy as np
from jax import lax
from jax.experimental import pallas as pl
from jax.experimental.pallas import tpu as pltpu
from jax.sharding import Mesh
from jax.sharding import PartitionSpec as P

TK = 128
KZ = 384
LANES = 128


def halves_of(table):
    high = table.astype(ml_dtypes.bfloat16)
    low = (table - high.astype(np.float64)).astype(ml_dtypes.bfloat16)
    return np.stack([high, low])


def dft_table(length, scale, start=0, step=1):
    n = np.arange(length // step)
    phase = ((start + step * n[:, None]) * n[None, :]) % length
    angle = phase * (2.0 * math.pi / length)
    cosine, sine = np.cos(angle) / scale, np.sin(angle) / scale
    return halves_of(np.block([[cosine, sine], [-sine, cosine]]))


def residue_tables(length):
    return np.stack([dft_table(length, math.sqrt(length), r, 4) for r in range(4)])


def turn(phase, length):
    shifted = (phase & (length - 1)) + length // 8
    quadrant = (shifted >> ((length // 4).bit_length() - 1)) & 3
    angle = ((shifted & (length // 4 - 1)) - length // 8).astype(jnp.float32) * (2.0 * math.pi / length)
    square = angle * angle
    sine = 1.0 / 362880
    for term in (-1.0 / 5040, 1.0 / 120, -1.0 / 6, 1.0):
        sine = sine * square + term
    sine = sine * angle
    cosine = 1.0 / 40320
    for term in (-1.0 / 720, 1.0 / 24, -0.5, 1.0):
        cosine = cosine * square + term
    swapped = (quadrant & 1) == 1
    first = jnp.where(swapped, sine, cosine)
    second = jnp.where(swapped, cosine, sine)
    first = jnp.where(((quadrant + 1) & 2) == 2, -first, first)
    second = jnp.where((quadrant & 2) == 2, -second, second)
    return first, second


def inverse_table(length):
    index = np.arange(length)
    angle = (index[:, None] * index[None, :] % length) * (2.0 * math.pi / length)
    return halves_of(np.concatenate([np.cos(angle), np.sin(angle)], axis=1) / math.sqrt(length))


def split(value):
    high = value.astype(jnp.bfloat16)
    low = (value - high.astype(jnp.float32)).astype(jnp.bfloat16)
    return high, low


def dot3(left, right, contract=((1,), (0,))):
    one = functools.partial(lax.dot_general, dimension_numbers=(contract, ((), ())), preferred_element_type=jnp.float32)
    return one(left[0], right[0]) + (one(left[1], right[0]) + one(left[0], right[1]))


def radix4(pieces):
    (ar, ai), (br, bi), (cr, ci), (dr, di) = pieces
    even = (ar + cr, ai + ci)
    odd = (br + dr, bi + di)
    even_less = (ar - cr, ai - ci)
    odd_less = (br - dr, bi - di)
    return [
        (even[0] + odd[0], even[1] + odd[1]),
        (even_less[0] + odd_less[1], even_less[1] - odd_less[0]),
        (even[0] - odd[0], even[1] - odd[1]),
        (even_less[0] - odd_less[1], even_less[1] + odd_less[0]),
    ]


def radix8(pieces):
    root = math.sqrt(0.5)
    evens, odds = radix4(pieces[0::2]), radix4(pieces[1::2])
    (ar, ai), (br, bi), (cr, ci), (dr, di) = odds
    turned = [(ar, ai), ((br + bi) * root, (bi - br) * root), (ci, -cr), ((di - dr) * root, -(dr + di) * root)]
    return [(e[0] + o[0], e[1] + o[1]) for e, o in zip(evens, turned)] + [
        (e[0] - o[0], e[1] - o[1]) for e, o in zip(evens, turned)
    ]


def weights_kernel(starts_ref, ids_ref, table_ref, inverse_ref, y_ref, out_ref, high_ref, low_ref):
    step = pl.program_id(0)
    block_count, freq_count, _ = table_ref.shape
    tiles = out_ref.shape[0]

    @pl.when(step == 0)
    def _():
        for w in range(block_count):
            high_ref[w], low_ref[w] = split(table_ref[w])

    @pl.when(step < pl.num_programs(0) - 1)
    def _():
        for t in range(tiles):
            tile = step * tiles + t
            first, second = ids_ref[2 * tile], ids_ref[2 * tile + 1]
            left = (
                jnp.concatenate([high_ref[first], high_ref[second]], axis=1),
                jnp.concatenate([low_ref[first], low_ref[second]], axis=1),
            )
            rows = pl.ds(pl.multiple_of(starts_ref[tile] * LANES, LANES), 2 * LANES)
            product = dot3(left, (inverse_ref[0, rows, :], inverse_ref[1, rows, :]))
            high, low = split(product)
            for h, half in enumerate((high, low)):
                for c in range(2):
                    out_ref[t, h, c * freq_count : (c + 1) * freq_count, :] = half[:, c * KZ : (c + 1) * KZ]

    @pl.when(step == pl.num_programs(0) - 1)
    def _():
        width = y_ref.shape[3]
        out_ref[:, :, :, :width] = y_ref[...]
        out_ref[:, :, :, width:] = jnp.zeros_like(out_ref[:, :, :, width:])


def tile_weights(stolt_table, kz_start, weight_ids):
    block_count, freq_count, block_width = stolt_table.shape
    kx_rows, tiles = kz_start.shape
    inverse = inverse_table(KZ)
    residues = residue_tables(tiles * TK)
    return pl.pallas_call(
        weights_kernel,
        grid_spec=pltpu.PrefetchScalarGridSpec(
            num_scalar_prefetch=2,
            grid=(kx_rows + 1,),
            in_specs=[
                pl.BlockSpec(stolt_table.shape, lambda i, *_: (0, 0, 0)),
                pl.BlockSpec(inverse.shape, lambda i, *_: (0, 0, 0)),
                pl.BlockSpec(residues.shape, lambda i, *_: (0, 0, 0, 0)),
            ],
            out_specs=pl.BlockSpec((tiles, 2, 2 * freq_count, KZ), lambda i, *_: (i, 0, 0, 0)),
            scratch_shapes=[pltpu.VMEM(stolt_table.shape, jnp.bfloat16)] * 2,
        ),
        out_shape=jax.ShapeDtypeStruct(((kx_rows + 1) * tiles, 2, 2 * freq_count, KZ), jnp.bfloat16),
        compiler_params=pltpu.CompilerParams(vmem_limit_bytes=24 << 20),
        name="tile_weights",
    )(kz_start.reshape(-1), weight_ids.reshape(-1), stolt_table, jnp.asarray(inverse), jnp.asarray(residues))


def forward_x_kernel(order, slots, x_ref, out_ref):
    sources, freqs, _, span, _ = x_ref.shape
    per = sources // 8
    piece = per * span
    pieces = []
    for q in range(8):
        pieces.append(
            tuple(
                jnp.concatenate(
                    [jnp.concatenate([x_ref[slot, f, c] for slot in slots[q * per : (q + 1) * per]], axis=0) for f in range(freqs)],
                    axis=1,
                )
                for c in range(2)
            )
        )
    row = lax.broadcasted_iota(jnp.int32, (piece, piece), 0)
    n = lax.broadcasted_iota(jnp.int32, (piece, piece), 1)
    k = sum(((row >> shift) & (size - 1)) * stride for shift, size, stride in order)
    cosine, sine = turn(k * n, piece)
    scale = 1.0 / math.sqrt(8 * piece)
    (cos_high, cos_low), (sin_high, sin_low) = split(cosine * scale), split(sine * scale)
    table = tuple(
        jnp.concatenate([jnp.concatenate([c, s], axis=1), jnp.concatenate([-s, c], axis=1)], axis=0)
        for c, s in ((cos_high, sin_high), (cos_low, sin_low))
    )
    column = lax.broadcasted_iota(jnp.int32, (piece, LANES), 1)
    cosines, sines = turn(lax.broadcasted_iota(jnp.int32, (piece, LANES), 0) * column, 8 * piece)
    lines = []
    for r, (real, imag) in enumerate(radix8(pieces)):
        if r > 0:
            cosine, sine = cosines[:, r : r + 1], sines[:, r : r + 1]
            real, imag = real * cosine + imag * sine, imag * cosine - real * sine
        product = dot3(table, split(jnp.concatenate([real, imag], axis=0)))
        lines += [
            product[c * piece : (c + 1) * piece, f * LANES : (f + 1) * LANES] for c in range(2) for f in range(freqs)
        ]
        if r % 4 == 3:
            order_out = [(row * 2 + c) * freqs + f for c in range(2) for row in range(4) for f in range(freqs)]
            out_ref[:, r // 4] = jnp.swapaxes(jnp.stack([lines[line] for line in order_out]), 0, 1)
            lines = []


def forward_x(received, order, slots):
    sources, freqs, _, span, columns = received.shape
    return pl.pallas_call(
        functools.partial(forward_x_kernel, order, slots),
        out_shape=jax.ShapeDtypeStruct((sources * span // 8, 2, 8 * freqs, columns), jnp.float32),
        compiler_params=pltpu.CompilerParams(vmem_limit_bytes=24 << 20),
        name="forward_x",
    )(received)


def image_kernel(before, s_ref, w_ref, out_ref, spec_ref, stage_ref, out_sems):
    _, kx_rows, ky_count, freq_count = spec_ref.shape
    tiles = ky_count // TK
    message = 4 * kx_rows
    y_tables = w_ref.shape[0] - 4
    y_width = ky_count // 2
    sources = s_ref.shape[0] // (4 * message)
    whole = s_ref[...].reshape(before, 4, sources // before, 2, message // 2, LANES)
    turned = [
        [jnp.swapaxes(whole[:, q, :, c].reshape(sources, message // 2, LANES), 0, 1) for c in range(2)] for q in range(4)
    ]
    for pair in range(0, kx_rows, 2):
        halves = [[] for _ in range(4)]
        for r in range(pair, pair + 2):
            pieces = []
            for q in range(4):
                parts = []
                for c in range(2):
                    rows = turned[q][c]
                    parts.append(jnp.concatenate([rows[r * 2], rows[r * 2 + 1]], axis=0))
                pieces.append(tuple(parts))
            for residue, (real, imag) in enumerate(radix4(pieces)):
                halves[residue].append(split(jnp.concatenate([real, imag], axis=1)))
        for residue in range(4):
            right = tuple(jnp.concatenate([pair_of[h] for pair_of in halves[residue]], axis=0) for h in range(2))
            table = tuple(w_ref[y_tables + residue, h, :, :y_width] for h in range(2))
            product = dot3(table, right, ((1,), (1,)))
            for c in range(2):
                for j in range(2):
                    spec_ref[c, pair + j, pl.ds(residue, ky_count // 4, stride=4), :] = product[
                        c * ky_count // 4 : (c + 1) * ky_count // 4, j * freq_count : (j + 1) * freq_count
                    ]

    copies = []
    for r in range(kx_rows):
        for t in range(tiles):
            rows = slice(t * TK, (t + 1) * TK)
            real = split(spec_ref[0, r, rows, :])
            imag = split(spec_ref[1, r, rows, :])
            left = tuple(jnp.concatenate([real[h], imag[h]], axis=1) for h in range(2))
            tile = r * tiles + t
            right = tuple(
                jnp.concatenate(
                    [
                        jnp.concatenate([w_ref[tile, h, :freq_count], w_ref[tile, h, freq_count:]], axis=1),
                        jnp.concatenate([-w_ref[tile, h, freq_count:], w_ref[tile, h, :freq_count]], axis=1),
                    ],
                    axis=0,
                )
                for h in range(2)
            )
            product = dot3(left, right)
            for c in range(2):
                stage_ref[c, r, rows, :] = product[:, c * KZ : (c + 1) * KZ]
            at = (slice(None), r, pl.ds(t * TK, TK), slice(None))
            copies.append(pltpu.make_async_copy(stage_ref.at[at], out_ref.at[at], out_sems.at[tile]))
            copies[-1].start()
    for copy in copies:
        copy.wait()


def form_image(columns, weights, kx_rows, before):
    tiles = weights.shape[0] // (kx_rows + 1)
    freq_count = weights.shape[2] // 2
    ky_count = tiles * TK
    shape = (2, kx_rows, ky_count, KZ)
    return pl.pallas_call(
        functools.partial(image_kernel, before),
        out_specs=pl.BlockSpec(memory_space=pltpu.HBM),
        scratch_shapes=[
            pltpu.VMEM((2, kx_rows, ky_count, freq_count), jnp.float32),
            pltpu.VMEM(shape, jnp.float32),
            pltpu.SemaphoreType.DMA((kx_rows * tiles,)),
        ],
        out_shape=jax.ShapeDtypeStruct(shape, jnp.float32),
        compiler_params=pltpu.CompilerParams(vmem_limit_bytes=28 << 20),
        name="form_image",
    )(columns, weights)


APERTURE_X = ("y", "z_lo", "core")
KX = ("x", "y", "z_lo", "core", "z_hi")
FIRST = ("y", "core", "z_lo")
SECOND = ("core", "y", "z_lo", "x", "z_hi")


def strides(axes, sizes):
    result, stride = {}, 1
    for axis in reversed(axes):
        result[axis] = stride
        stride *= sizes[axis]
    return result


def product_of(axes, sizes):
    return math.prod(sizes[axis] for axis in axes)


def shards(echoes, stolt_table, kz_start, weight_ids):
    sizes = {axis: lax.axis_size(axis) for axis in KX}
    count_ax = product_of(FIRST, sizes)
    freqs, _, span, columns = echoes.shape
    share = freqs // count_ax
    outgoing = echoes.reshape(count_ax, share, 2, span, columns)
    received = lax.all_to_all(outgoing, FIRST, split_axis=0, concat_axis=0, tiled=True)

    blocks, freq_count, width = stolt_table.shape
    held = ("z_hi",) + FIRST
    arriving = [axis for axis in SECOND if axis != "x"]
    ordered = stolt_table.reshape((blocks,) + tuple(sizes[axis] for axis in held) + (share, width))
    ordered = ordered.transpose([0, len(held) + 1] + [1 + held.index(axis) for axis in arriving] + [len(held) + 2])
    weights = tile_weights(ordered.reshape(blocks, freq_count, width), kz_start, weight_ids)

    in_slot = strides(FIRST, sizes)
    grid = np.indices([sizes[axis] for axis in APERTURE_X]).reshape(len(APERTURE_X), -1)
    slots = [int(slot) for slot in sum(grid[i] * in_slot[axis] for i, axis in enumerate(APERTURE_X))]
    in_row, in_kx = strides(SECOND[:-1], sizes), strides(KX[:-1], sizes)
    order = [(in_row[axis].bit_length() - 1, sizes[axis], in_kx[axis]) for axis in in_kx]
    spectrum = forward_x(received, order, slots)
    spectrum, weights = lax.optimization_barrier((spectrum, weights))
    messages = spectrum.reshape(product_of(SECOND, sizes), -1, columns)
    gathered = lax.all_to_all(messages, SECOND, split_axis=0, concat_axis=0, tiled=True)
    before = product_of(SECOND[: SECOND.index("x")], sizes)
    return form_image(gathered.reshape(-1, columns), weights, kz_start.shape[0], before)


def solution(mesh):
    y, z_lo, core = 4, 4, 2
    fine = Mesh(
        mesh.devices.reshape(y, z_lo, core, mesh.shape["ay"], mesh.shape["fr"]), ("y", "z_lo", "core", "x", "z_hi")
    )
    placed = (
        P("z_hi", None, APERTURE_X, "x"),
        P(),
        P(KX, None),
        P(KX, None, None),
    )
    return jax.shard_map(
        shards,
        mesh=fine,
        in_specs=placed,
        out_specs=P(None, KX, None, None),
        check_vma=False,
    )
```

```python
import functools
import math

import jax
import jax.numpy as jnp
import ml_dtypes
import numpy as np
from jax import lax
from jax.experimental import pallas as pl
from jax.experimental.pallas import tpu as pltpu
from jax.sharding import Mesh
from jax.sharding import PartitionSpec as P

TK = 128
KZ = 384
LANES = 128


def halves_of(table):
    high = table.astype(ml_dtypes.bfloat16)
    low = (table - high.astype(np.float64)).astype(ml_dtypes.bfloat16)
    return np.stack([high, low])


def dft_table(length, scale, start=0, step=1):
    n = np.arange(length // step)
    phase = ((start + step * n[:, None]) * n[None, :]) % length
    angle = phase * (2.0 * math.pi / length)
    cosine, sine = np.cos(angle) / scale, np.sin(angle) / scale
    return halves_of(np.block([[cosine, sine], [-sine, cosine]]))


def residue_tables(length):
    return np.stack([dft_table(length, math.sqrt(length), r, 4) for r in range(4)])


def turn(phase, length):
    shifted = (phase & (length - 1)) + length // 8
    quadrant = (shifted >> ((length // 4).bit_length() - 1)) & 3
    angle = ((shifted & (length // 4 - 1)) - length // 8).astype(jnp.float32) * (2.0 * math.pi / length)
    square = angle * angle
    sine = 1.0 / 362880
    for term in (-1.0 / 5040, 1.0 / 120, -1.0 / 6, 1.0):
        sine = sine * square + term
    sine = sine * angle
    cosine = 1.0 / 40320
    for term in (-1.0 / 720, 1.0 / 24, -0.5, 1.0):
        cosine = cosine * square + term
    swapped = (quadrant & 1) == 1
    first = jnp.where(swapped, sine, cosine)
    second = jnp.where(swapped, cosine, sine)
    first = jnp.where(((quadrant + 1) & 2) == 2, -first, first)
    second = jnp.where((quadrant & 2) == 2, -second, second)
    return first, second


def inverse_table(length):
    index = np.arange(length)
    angle = (index[:, None] * index[None, :] % length) * (2.0 * math.pi / length)
    return halves_of(np.concatenate([np.cos(angle), np.sin(angle)], axis=1) / math.sqrt(length))


def split(value):
    high = value.astype(jnp.bfloat16)
    low = (value - high.astype(jnp.float32)).astype(jnp.bfloat16)
    return high, low


def dot3(left, right, contract=((1,), (0,))):
    one = functools.partial(lax.dot_general, dimension_numbers=(contract, ((), ())), preferred_element_type=jnp.float32)
    return one(left[0], right[0]) + (one(left[1], right[0]) + one(left[0], right[1]))


def radix4(pieces):
    (ar, ai), (br, bi), (cr, ci), (dr, di) = pieces
    even = (ar + cr, ai + ci)
    odd = (br + dr, bi + di)
    even_less = (ar - cr, ai - ci)
    odd_less = (br - dr, bi - di)
    return [
        (even[0] + odd[0], even[1] + odd[1]),
        (even_less[0] + odd_less[1], even_less[1] - odd_less[0]),
        (even[0] - odd[0], even[1] - odd[1]),
        (even_less[0] - odd_less[1], even_less[1] + odd_less[0]),
    ]


def radix8(pieces):
    root = math.sqrt(0.5)
    evens, odds = radix4(pieces[0::2]), radix4(pieces[1::2])
    (ar, ai), (br, bi), (cr, ci), (dr, di) = odds
    turned = [(ar, ai), ((br + bi) * root, (bi - br) * root), (ci, -cr), ((di - dr) * root, -(dr + di) * root)]
    return [(e[0] + o[0], e[1] + o[1]) for e, o in zip(evens, turned)] + [
        (e[0] - o[0], e[1] - o[1]) for e, o in zip(evens, turned)
    ]


def weights_kernel(starts_ref, ids_ref, table_ref, inverse_ref, y_ref, out_ref, high_ref, low_ref):
    step = pl.program_id(0)
    block_count, freq_count, _ = table_ref.shape
    tiles = out_ref.shape[0]

    @pl.when(step == 0)
    def _():
        for w in range(block_count):
            high_ref[w], low_ref[w] = split(table_ref[w])

    @pl.when(step < pl.num_programs(0) - 1)
    def _():
        for t in range(tiles):
            tile = step * tiles + t
            first, second = ids_ref[2 * tile], ids_ref[2 * tile + 1]
            left = (
                jnp.concatenate([high_ref[first], high_ref[second]], axis=1),
                jnp.concatenate([low_ref[first], low_ref[second]], axis=1),
            )
            rows = pl.ds(pl.multiple_of(starts_ref[tile] * LANES, LANES), 2 * LANES)
            product = dot3(left, (inverse_ref[0, rows, :], inverse_ref[1, rows, :]))
            high, low = split(product)
            for h, half in enumerate((high, low)):
                for c in range(2):
                    out_ref[t, h, c * freq_count : (c + 1) * freq_count, :] = half[:, c * KZ : (c + 1) * KZ]

    @pl.when(step == pl.num_programs(0) - 1)
    def _():
        width = y_ref.shape[3]
        out_ref[:, :, :, :width] = y_ref[...]
        out_ref[:, :, :, width:] = jnp.zeros_like(out_ref[:, :, :, width:])


def tile_weights(stolt_table, kz_start, weight_ids):
    block_count, freq_count, block_width = stolt_table.shape
    kx_rows, tiles = kz_start.shape
    inverse = inverse_table(KZ)
    residues = residue_tables(tiles * TK)
    return pl.pallas_call(
        weights_kernel,
        grid_spec=pltpu.PrefetchScalarGridSpec(
            num_scalar_prefetch=2,
            grid=(kx_rows + 1,),
            in_specs=[
                pl.BlockSpec(stolt_table.shape, lambda i, *_: (0, 0, 0)),
                pl.BlockSpec(inverse.shape, lambda i, *_: (0, 0, 0)),
                pl.BlockSpec(residues.shape, lambda i, *_: (0, 0, 0, 0)),
            ],
            out_specs=pl.BlockSpec((tiles, 2, 2 * freq_count, KZ), lambda i, *_: (i, 0, 0, 0)),
            scratch_shapes=[pltpu.VMEM(stolt_table.shape, jnp.bfloat16)] * 2,
        ),
        out_shape=jax.ShapeDtypeStruct(((kx_rows + 1) * tiles, 2, 2 * freq_count, KZ), jnp.bfloat16),
        compiler_params=pltpu.CompilerParams(vmem_limit_bytes=24 << 20),
        name="tile_weights",
    )(kz_start.reshape(-1), weight_ids.reshape(-1), stolt_table, jnp.asarray(inverse), jnp.asarray(residues))


def forward_x_kernel(order, slots, x_ref, out_ref):
    sources, freqs, _, span, _ = x_ref.shape
    per = sources // 8
    piece = per * span
    pieces = []
    for q in range(8):
        pieces.append(
            tuple(
                jnp.concatenate(
                    [jnp.concatenate([x_ref[slot, f, c] for slot in slots[q * per : (q + 1) * per]], axis=0) for f in range(freqs)],
                    axis=1,
                )
                for c in range(2)
            )
        )
    row = lax.broadcasted_iota(jnp.int32, (piece, piece), 0)
    n = lax.broadcasted_iota(jnp.int32, (piece, piece), 1)
    k = sum(((row >> shift) & (size - 1)) * stride for shift, size, stride in order)
    cosine, sine = turn(k * n, piece)
    scale = 1.0 / math.sqrt(8 * piece)
    (cos_high, cos_low), (sin_high, sin_low) = split(cosine * scale), split(sine * scale)
    table = tuple(
        jnp.concatenate([jnp.concatenate([c, s], axis=1), jnp.concatenate([-s, c], axis=1)], axis=0)
        for c, s in ((cos_high, sin_high), (cos_low, sin_low))
    )
    column = lax.broadcasted_iota(jnp.int32, (piece, LANES), 1)
    cosines, sines = turn(lax.broadcasted_iota(jnp.int32, (piece, LANES), 0) * column, 8 * piece)
    lines = []
    for r, (real, imag) in enumerate(radix8(pieces)):
        if r > 0:
            cosine, sine = cosines[:, r : r + 1], sines[:, r : r + 1]
            real, imag = real * cosine + imag * sine, imag * cosine - real * sine
        product = dot3(table, split(jnp.concatenate([real, imag], axis=0)))
        lines += [
            product[c * piece : (c + 1) * piece, f * LANES : (f + 1) * LANES] for c in range(2) for f in range(freqs)
        ]
        if r % 4 == 3:
            order_out = [(row * 2 + c) * freqs + f for c in range(2) for row in range(4) for f in range(freqs)]
            out_ref[:, r // 4] = jnp.swapaxes(jnp.stack([lines[line] for line in order_out]), 0, 1)
            lines = []


def forward_x(received, order, slots):
    sources, freqs, _, span, columns = received.shape
    return pl.pallas_call(
        functools.partial(forward_x_kernel, order, slots),
        out_shape=jax.ShapeDtypeStruct((sources * span // 8, 2, 8 * freqs, columns), jnp.float32),
        compiler_params=pltpu.CompilerParams(vmem_limit_bytes=50 << 20),
        name="forward_x",
    )(received)


def image_kernel(before, s_ref, w_ref, out_ref, spec_ref, stage_ref, out_sems):
    _, kx_rows, ky_count, freq_count = spec_ref.shape
    tiles = ky_count // TK
    message = 4 * kx_rows
    y_tables = w_ref.shape[0] - 4
    y_width = ky_count // 2
    sources = s_ref.shape[0] // (4 * message)
    whole = s_ref[...].reshape(before, 4, sources // before, 2, message // 2, LANES)
    turned = [
        [jnp.swapaxes(whole[:, q, :, c].reshape(sources, message // 2, LANES), 0, 1) for c in range(2)] for q in range(4)
    ]
    for pair in range(0, kx_rows, 2):
        halves = [[] for _ in range(4)]
        for r in range(pair, pair + 2):
            pieces = []
            for q in range(4):
                parts = []
                for c in range(2):
                    rows = turned[q][c]
                    parts.append(jnp.concatenate([rows[r * 2], rows[r * 2 + 1]], axis=0))
                pieces.append(tuple(parts))
            for residue, (real, imag) in enumerate(radix4(pieces)):
                halves[residue].append(split(jnp.concatenate([real, imag], axis=1)))
        for residue in range(4):
            right = tuple(jnp.concatenate([pair_of[h] for pair_of in halves[residue]], axis=0) for h in range(2))
            table = tuple(w_ref[y_tables + residue, h, :, :y_width] for h in range(2))
            product = dot3(table, right, ((1,), (1,)))
            for c in range(2):
                for j in range(2):
                    spec_ref[c, pair + j, pl.ds(residue, ky_count // 4, stride=4), :] = product[
                        c * ky_count // 4 : (c + 1) * ky_count // 4, j * freq_count : (j + 1) * freq_count
                    ]

    copies = []
    for r in range(kx_rows):
        for t in range(tiles):
            rows = slice(t * TK, (t + 1) * TK)
            real = split(spec_ref[0, r, rows, :])
            imag = split(spec_ref[1, r, rows, :])
            left = tuple(jnp.concatenate([real[h], imag[h]], axis=1) for h in range(2))
            tile = r * tiles + t
            right = tuple(
                jnp.concatenate(
                    [
                        jnp.concatenate([w_ref[tile, h, :freq_count], w_ref[tile, h, freq_count:]], axis=1),
                        jnp.concatenate([-w_ref[tile, h, freq_count:], w_ref[tile, h, :freq_count]], axis=1),
                    ],
                    axis=0,
                )
                for h in range(2)
            )
            product = dot3(left, right)
            for c in range(2):
                stage_ref[c, r, rows, :] = product[:, c * KZ : (c + 1) * KZ]
            at = (slice(None), r, pl.ds(t * TK, TK), slice(None))
            copies.append(pltpu.make_async_copy(stage_ref.at[at], out_ref.at[at], out_sems.at[tile]))
            copies[-1].start()
    for copy in copies:
        copy.wait()


def form_image(columns, weights, kx_rows, before):
    tiles = weights.shape[0] // (kx_rows + 1)
    freq_count = weights.shape[2] // 2
    ky_count = tiles * TK
    shape = (2, kx_rows, ky_count, KZ)
    return pl.pallas_call(
        functools.partial(image_kernel, before),
        out_specs=pl.BlockSpec(memory_space=pltpu.HBM),
        scratch_shapes=[
            pltpu.VMEM((2, kx_rows, ky_count, freq_count), jnp.float32),
            pltpu.VMEM(shape, jnp.float32),
            pltpu.SemaphoreType.DMA((kx_rows * tiles,)),
        ],
        out_shape=jax.ShapeDtypeStruct(shape, jnp.float32),
        compiler_params=pltpu.CompilerParams(vmem_limit_bytes=28 << 20),
        name="form_image",
    )(columns, weights)


APERTURE_X = ("y", "z_lo", "core")
KX = ("x", "y", "z_lo", "core", "z_hi")
FIRST = ("y", "core", "z_lo")
SECOND = ("core", "y", "z_lo", "x", "z_hi")


def strides(axes, sizes):
    result, stride = {}, 1
    for axis in reversed(axes):
        result[axis] = stride
        stride *= sizes[axis]
    return result


def product_of(axes, sizes):
    return math.prod(sizes[axis] for axis in axes)


def shards(echoes, stolt_table, kz_start, weight_ids):
    sizes = {axis: lax.axis_size(axis) for axis in KX}
    count_ax = product_of(FIRST, sizes)
    freqs, _, span, columns = echoes.shape
    share = freqs // count_ax
    outgoing = echoes.reshape(count_ax, share, 2, span, columns)
    received = lax.all_to_all(outgoing, FIRST, split_axis=0, concat_axis=0, tiled=True)

    blocks, freq_count, width = stolt_table.shape
    held = ("z_hi",) + FIRST
    arriving = [axis for axis in SECOND if axis != "x"]
    ordered = stolt_table.reshape((blocks,) + tuple(sizes[axis] for axis in held) + (share, width))
    ordered = ordered.transpose([0, len(held) + 1] + [1 + held.index(axis) for axis in arriving] + [len(held) + 2])
    weights = tile_weights(ordered.reshape(blocks, freq_count, width), kz_start, weight_ids)

    in_slot = strides(FIRST, sizes)
    grid = np.indices([sizes[axis] for axis in APERTURE_X]).reshape(len(APERTURE_X), -1)
    slots = [int(slot) for slot in sum(grid[i] * in_slot[axis] for i, axis in enumerate(APERTURE_X))]
    in_row, in_kx = strides(SECOND[:-1], sizes), strides(KX[:-1], sizes)
    order = [(in_row[axis].bit_length() - 1, sizes[axis], in_kx[axis]) for axis in in_kx]
    spectrum = forward_x(received, order, slots)
    spectrum, weights = lax.optimization_barrier((spectrum, weights))
    messages = spectrum.reshape(product_of(SECOND, sizes), -1, columns)
    gathered = lax.all_to_all(messages, SECOND, split_axis=0, concat_axis=0, tiled=True)
    before = product_of(SECOND[: SECOND.index("x")], sizes)
    return form_image(gathered.reshape(-1, columns), weights, kz_start.shape[0], before)


def solution(mesh):
    y, z_lo, core = 4, 4, 2
    fine = Mesh(
        mesh.devices.reshape(y, z_lo, core, mesh.shape["ay"], mesh.shape["fr"]), ("y", "z_lo", "core", "x", "z_hi")
    )
    placed = (
        P("z_hi", None, APERTURE_X, "x"),
        P(),
        P(KX, None),
        P(KX, None, None),
    )
    return jax.shard_map(
        shards,
        mesh=fine,
        in_specs=placed,
        out_specs=P(None, KX, None, None),
        check_vma=False,
    )
```
